32 devices in a mesh: section: 4 (over y, x), dp: 8 (over z, core).
Axes of the slice: x: 2, y: 2, z: 4, core: 2. Of those that a mesh axis runs over, the one named last changes fastest.
Arguments:
- acts: bfloat16 [4, 4, 256, 4096], P('section', None, 'dp'), may hold values from -6 to 6
- grads_out: bfloat16 [4, 4, 256, 4096], P('section', None, 'dp'), may hold values from -6 to 6
- weight_grad: bfloat16 [4, 4096, 4096], P('section', 'dp'), may hold values from -16 to 16
- old_in_factor: float32 [4, 32, 128, 128], P('section', 'dp'), may hold values from -12 to 24, as said below
- old_out_factor: float32 [4, 32, 128, 128], P('section', 'dp'), may hold values from -12 to 24, as said below
Outputs:
- update: bfloat16 [4, 4096, 4096], P('section', 'dp')
- in_factor: float32 [4, 32, 128, 128], P('section', 'dp')
- out_factor: float32 [4, 32, 128, 128], P('section', 'dp')
The draws below stay inside these ranges and needn't reach their ends.
Inputs may be any that keep to these rules, and one draw needn't show every extreme that they name: `old_in_factor`: each block is symmetric positive definite. `old_out_factor`: each block is symmetric positive definite.
All inputs are finite; a program needn't handle non-finite values.
Results may differ from the reference program's by a relative error of at most 0.0064.
Values may be sent and summed in bfloat16 or wider, within the bound.
No kernel may reach another device: no remote copies, remote signals or barrier semaphores. Data moves between devices by JAX's collectives and lax.ppermute only.
A program may use at most 64 MiB of HBM per device.

```python
import jax
import jax.numpy as jnp
from jax import lax

D_IN = 4096
D_OUT = 4096
BLK = 128
MICRO = 4
ITERS = 8
TOKENS = 256
LAYERS = 4
NBLK_IN = 32
NBLK_OUT = 32


def spd_blocks(key, count, shared):
    normal_key = jax.random.fold_in(jax.random.fold_in(key, 7), 0)
    level_key = jax.random.fold_in(jax.random.fold_in(key, 7), 2)
    rough = jax.random.normal(normal_key, (LAYERS, count, BLK, 2 * BLK), jnp.float32)
    blocks = jnp.einsum('lbik,lbjk->lbij', rough, rough, precision=lax.Precision.HIGHEST) / (2 * BLK)
    if shared:
        levels = jnp.exp(jax.random.uniform(level_key, (1, count, 1, 1), jnp.float32, -1.4, 1.4))
    else:
        levels = jnp.exp(jax.random.uniform(level_key, (LAYERS, count, 1, 1), jnp.float32, -1.4, 1.4))
    return jnp.clip(blocks * levels, -12.0, 24.0)


def draw_old_in_factor(key, part):
    return spd_blocks(jax.random.fold_in(key, 11), NBLK_IN, False)


def draw_old_out_factor(key, part):
    return spd_blocks(jax.random.fold_in(key, 13), NBLK_OUT, True)


def draw_weight_grad(key, part):
    main_key = jax.random.fold_in(jax.random.fold_in(key, 17), 0)
    level_key = jax.random.fold_in(jax.random.fold_in(key, 17), 2)
    widest = max(NBLK_IN, NBLK_OUT)
    levels = jnp.exp(jax.random.uniform(level_key, (LAYERS, widest), jnp.float32, -0.85, 0.85))
    row_scale = jnp.repeat(levels[:, :NBLK_OUT], BLK, axis=1)
    col_scale = jnp.repeat(levels[:, :NBLK_IN], BLK, axis=1)
    values = jax.random.normal(main_key, (LAYERS, D_OUT, D_IN), jnp.float32)
    scaled = values * row_scale[:, :, None] * col_scale[:, None, :]
    return jnp.clip(scaled, -16.0, 16.0).astype(jnp.bfloat16)


def block_levels(stream_key, dims, cuts, smallest, top_value):
    def one(axis_at, parts):
        draws = jax.random.uniform(jax.random.fold_in(jax.random.fold_in(stream_key, 6), axis_at), (parts,), jnp.float32, smallest / len(cuts), top_value / len(cuts))
        return jnp.repeat(jnp.exp(draws), dims[axis_at] // parts).reshape((-1,) + (1,) * (len(dims) - axis_at - 1))

    factor_of = one(*cuts[0])
    for cut in cuts[1:]:
        factor_of = factor_of * one(*cut)
    return factor_of


def centred(own_key, extent, spread, bound, cuts=(), kind=jnp.bfloat16):
    gain = block_levels(own_key, extent, cuts, -0.22, 0.18) if cuts else 1.0
    result = jax.random.normal(own_key, extent, jnp.float32) * spread * gain
    return jnp.minimum(jnp.maximum(result, -bound), bound).astype(kind)


def setup_inputs(seed: int = 0) -> dict:
    streams_of = jax.random.split(jax.random.key(seed), 6)
    return {
        "acts": centred(streams_of[0], (LAYERS, MICRO, TOKENS, D_IN), 1.0, 6.0, ((0, 4), (2, 8))),
        "grads_out": centred(streams_of[1], (LAYERS, MICRO, TOKENS, D_OUT), 1.0, 6.0, ((0, 4), (2, 8))),
        "weight_grad": draw_weight_grad(jax.random.fold_in(streams_of[5], 71), 0),
        "old_in_factor": draw_old_in_factor(jax.random.fold_in(streams_of[5], 71), 0),
        "old_out_factor": draw_old_out_factor(jax.random.fold_in(streams_of[5], 71), 0),
    }


DECAY = 0.7
DAMPING = 0.1
CLIP = 0.04
HIGH = lax.Precision.HIGHEST

def newton(factor):
    size = factor.shape[-1]
    eye = jnp.eye(size, dtype=jnp.float32)
    damped = factor + DAMPING * eye
    norms = jnp.sqrt(lax.optimization_barrier(jnp.sum(damped * damped, axis=(1, 2))))
    approx = eye[None] / norms[:, None, None]
    for sweep in range(ITERS):
        product = jnp.einsum('bij,bjk->bik', damped, approx, precision=HIGH)
        approx = jnp.einsum('bij,bjk->bik', approx, 2.0 * eye - product, precision=HIGH)
    return approx

def one_layer(items):
    acts_l, grads_l, wgrad_l, old_in, old_out = items
    count = MICRO * TOKENS
    flat_in = acts_l.reshape(-1, NBLK_IN, BLK).astype(jnp.float32)
    flat_out = grads_l.reshape(-1, NBLK_OUT, BLK).astype(jnp.float32)
    gram_in = jnp.einsum('tbi,tbj->bij', flat_in, flat_in, precision=HIGH) / count
    gram_out = jnp.einsum('tbi,tbj->bij', flat_out, flat_out, precision=HIGH) / count
    in_factor = DECAY * old_in + (1.0 - DECAY) * gram_in
    out_factor = DECAY * old_out + (1.0 - DECAY) * gram_out
    in_inverse = newton(in_factor).astype(jnp.bfloat16)
    out_inverse = newton(out_factor).astype(jnp.bfloat16)
    blocks = wgrad_l.reshape(NBLK_OUT, BLK, D_IN).astype(jnp.float32)
    left = jnp.einsum('bij,bjd->bid', out_inverse.astype(jnp.float32), blocks, precision=HIGH)
    left = left.astype(jnp.bfloat16).reshape(D_OUT, NBLK_IN, BLK)
    natural = jnp.einsum('rci,cij->rcj', left.astype(jnp.float32), in_inverse.astype(jnp.float32), precision=HIGH)
    natural = natural.reshape(D_OUT, D_IN)
    quad_part = jnp.sum(natural * wgrad_l.astype(jnp.float32))
    return (natural, quad_part, in_factor, out_factor)

def reference(acts, grads_out, weight_grad, old_in_factor, old_out_factor):
    natural, quad_parts, in_factor, out_factor = lax.map(one_layer, (acts, grads_out, weight_grad, old_in_factor, old_out_factor))
    quad = jnp.sum(quad_parts)
    numel = LAYERS * D_OUT * D_IN
    scale = jnp.minimum(1.0, jnp.sqrt(CLIP * numel / quad))
    update = (scale * natural).astype(jnp.bfloat16)
    return (update, in_factor, out_factor)
```

```python
import functools
import math

import jax
import jax.numpy as jnp
from jax import lax
from jax.experimental import pallas as pl
from jax.experimental.pallas import tpu as pltpu
from jax.sharding import PartitionSpec as P

ITERS = 8
DECAY = 0.7
DAMPING = 0.1
CLIP = 0.04
F32 = jnp.float32
BF16 = jnp.bfloat16
VMEM = pl.BlockSpec(memory_space=pltpu.VMEM)


def pairs_of(count):
    pairs = [(b, b + 1) for b in range(0, count - 1, 2)]
    return pairs + ([(count - 1, None)] if count % 2 else [])


def message_rows(count, block):
    pairs = len(pairs_of(count))
    return pairs * block + -(-pairs // 16) * 16


def grid_of(block):
    rows = lax.broadcasted_iota(jnp.int32, (block, block), 0)
    cols = lax.broadcasted_iota(jnp.int32, (block, block), 1)
    return rows, cols


def contract_rows(a, b):
    return lax.dot_general(a, b, (((0,), (0,)), ((), ())), preferred_element_type=F32)


def dot(a, b):
    return jnp.dot(a, b, preferred_element_type=F32)


def store_packed(ref, blocks, block):
    rows, cols = grid_of(block)
    pairs = pairs_of(len(blocks))
    height = len(pairs) * block
    lines = []
    for at, (a, b) in enumerate(pairs):
        first = blocks[a]
        if b is None:
            joined = first
            lines.append(jnp.zeros((1, block), F32))
        else:
            joined = jnp.where(rows < cols, first, blocks[b])
            lines.append(jnp.sum(jnp.where(rows == cols, first, 0.0), axis=0, keepdims=True))
        ref[at * block:(at + 1) * block, :] = joined.astype(ref.dtype)
    extra = ref.shape[0] - height
    tail = jnp.zeros((extra, block), F32)
    spot = lax.broadcasted_iota(jnp.int32, (extra, block), 0)
    for at, line in enumerate(lines):
        tail = jnp.where(spot == at, line, tail)
    ref[height:, :] = tail.astype(ref.dtype)


def unpacked(packed, count, block):
    rows, cols = grid_of(block)
    pairs = pairs_of(count)
    height = len(pairs) * block
    blocks = []
    for at, (a, b) in enumerate(pairs):
        joined = packed[at * block:(at + 1) * block]
        if b is None:
            blocks.append(joined)
            continue
        flipped = joined.T
        line = packed[height + at:height + at + 1]
        blocks.append(jnp.where(rows == cols, line, jnp.where(rows < cols, joined, flipped)))
        blocks.append(jnp.where(rows < cols, flipped, joined))
    return blocks


def gram_kernel(chips, count, block, own_ref, other_ref, *out_refs):
    place = lax.axis_index("dp")
    chip, core = place // 2, place % 2
    wide = count * block
    for step in range(chips):
        owner = lax.rem(chip + step, chips) * 2 + core
        cols = pl.ds(pl.multiple_of(owner * wide, wide), wide)
        tokens = jnp.concatenate([
            ref[m, :, cols] for ref in (own_ref, other_ref) for m in range(own_ref.shape[0])
        ], axis=0)
        grams = []
        for b in range(count):
            part = tokens[:, b * block:(b + 1) * block]
            grams.append(contract_rows(part, part))
        store_packed(out_refs[step], grams, block)


def halves(x):
    high = x.astype(BF16)
    return high, (x - high.astype(F32)).astype(BF16)


def inverses(damped, block):
    rows, cols = grid_of(block)
    eye2 = jnp.where(rows == cols, 2.0, 0.0)
    norms = [jnp.sqrt(jnp.sum(m * m, axis=(0, 1), keepdims=True)) for m in damped]
    ys = [m / n for m, n in zip(damped, norms)]
    xs = [eye2 - y for y in ys]
    for stage in range(ITERS):
        parts = [halves(y) for y in ys]
        lefts = []
        for x, (high, low) in zip(xs, parts):
            if stage == 0:
                lefts.append((high, low))
                continue
            x_high, x_low = halves(x)
            if stage == ITERS - 1:
                lefts.append((x_high, x_low))
            else:
                lefts.append((jnp.concatenate([x_high, high], 0), jnp.concatenate([x_low, low], 0)))
        prods = []
        for (lhigh, llow), (high, low) in zip(lefts, parts):
            both = jnp.concatenate([lhigh, llow], 1)
            prods.append(dot(both, jnp.concatenate([high, high], 0)) + dot(lhigh, low))
        if stage == 0:
            ys = [2.0 * y - p for y, p in zip(ys, prods)]
        elif stage == ITERS - 1:
            xs = [2.0 * x - p for x, p in zip(xs, prods)]
        else:
            xs = [2.0 * x - p[:block] for x, p in zip(xs, prods)]
            ys = [2.0 * y - p[block:] for y, p in zip(ys, prods)]
    return [x / n for x, n in zip(xs, norms)]


def factor_kernel(tokens, packed, count, block, *refs):
    sums, (old_ref, factor_ref, inverse_ref) = refs[:-3], refs[-3:]
    total = sums[0][...]
    for ref in sums[1:]:
        total = total + ref[...].astype(F32)
    rows, cols = grid_of(block)
    damped = []
    for b, gram in enumerate(unpacked(total, count, block)):
        factor = DECAY * old_ref[b] + ((1.0 - DECAY) / tokens) * gram
        factor_ref[b] = factor
        damped.append(factor + jnp.where(rows == cols, DAMPING, 0.0))
    results = inverses(damped, block)
    if packed:
        store_packed(inverse_ref, results, block)
    else:
        for b in range(count):
            inverse_ref[b] = results[b].astype(BF16)


def left_kernel(count, block, inverse_ref, grad_ref, left_ref, fold_ref):
    outs = inverse_ref.shape[0]
    rows, cols = grid_of(block)
    grad = grad_ref[...]
    left = jnp.concatenate([
        dot(inverse_ref[b], grad[b * block:(b + 1) * block]).astype(BF16) for b in range(outs)
    ], axis=0)
    left_ref[...] = left
    sums = []
    for c in range(count):
        span = slice(c * block, (c + 1) * block)
        sums.append(contract_rows(left[:, span], grad[:, span]))
    pairs = pairs_of(count)
    height = len(pairs) * block
    extra = fold_ref.shape[1] - height
    tail = jnp.zeros((extra, block), F32)
    spot = lax.broadcasted_iota(jnp.int32, (extra, block), 0)
    for at, (a, b) in enumerate(pairs):
        first = sums[a]
        if b is None:
            fold_ref[0, at * block:(at + 1) * block, :] = first
            continue
        second = sums[b]
        fold_ref[0, at * block:(at + 1) * block, :] = jnp.where(
            rows < cols, first + first.T, second + jnp.where(rows > cols, second.T, 0.0)
        )
        line = jnp.sum(jnp.where(rows == cols, first, 0.0), axis=0, keepdims=True)
        tail = jnp.where(spot == at, line, tail)
    fold_ref[0, height:, :] = tail


def owner_of(index, chips):
    place = lax.axis_index("dp")
    chip, core = place // 2, place % 2
    side, step = index // chips, index % chips
    return lax.rem(chip + chips - step, chips) * 2 + (core if side == 0 else 1 - core)


def quad_kernel(chips, *refs):
    messages, (fold_ref, out_ref) = refs[:-2], refs[-2:]
    total = None
    for index, ref in enumerate(messages):
        term = ref[...].astype(F32) * fold_ref[owner_of(index, chips)]
        total = term if total is None else total + term
    out_ref[...] = jnp.broadcast_to(jnp.sum(total, axis=(0, 1), keepdims=True), out_ref.shape)


def natural_kernel(chips, count, block, *refs):
    messages, (left_ref, out_ref) = refs[:-2], refs[-2:]
    for index, ref in enumerate(messages):
        start = owner_of(index, chips) * (count * block)
        for b, inverse in enumerate(unpacked(ref[...].astype(F32), count, block)):
            cols = pl.ds(pl.multiple_of(start + b * block, block), block)
            out_ref[:, cols] = dot(left_ref[:, cols], inverse.astype(BF16))


def scale_kernel(numel, *refs):
    sums, (natural_ref, out_ref) = refs[:-2], refs[-2:]
    quad = sums[0][...]
    for ref in sums[1:]:
        quad = quad + ref[...]
    scale = jnp.minimum(1.0, jnp.sqrt(CLIP * numel / quad))[0:1, 0:1]
    tall = out_ref.shape[0]
    rows = pl.ds(pl.multiple_of(pl.program_id(0) * tall, tall), tall)
    out_ref[...] = (scale * natural_ref[rows, :]).astype(BF16)


def cost(flops, size):
    return pl.CostEstimate(flops=int(flops), bytes_accessed=int(size), transcendentals=0)


def params(mib):
    return pltpu.CompilerParams(vmem_limit_bytes=mib << 20)


def shaped(shape, dtype):
    return jax.ShapeDtypeStruct(shape, dtype)


def body(acts, grads_out, weight_grad, old_in_factor, old_out_factor):
    groups = lax.axis_size("dp")
    sections = lax.axis_size("section")
    chips = groups // 2
    block = old_in_factor.shape[-1]
    rows, width = weight_grad.shape[1:]
    tokens = acts.shape[1] * acts.shape[2] * groups

    swap = [(i, i ^ 1) for i in range(groups)]

    def ahead(step):
        return [(c * 2 + core, ((c + step) % chips) * 2 + core) for c in range(chips) for core in range(2)]

    def block_sums(values, count):
        other = lax.ppermute(values, "dp", swap)
        shape = (message_rows(count, block), block)
        sums = pl.pallas_call(
            functools.partial(gram_kernel, chips, count, block),
            out_shape=[shaped(shape, F32)] * chips,
            in_specs=[VMEM] * 2,
            out_specs=[VMEM] * chips,
            compiler_params=params(24),
            cost_estimate=cost(2 * tokens * block * width // chips, 4 * values.size),
            name="gram",
        )(values[0], other[0])
        return [sums[0]] + [lax.ppermute(sums[k], "dp", ahead(k)) for k in range(1, chips)]

    def factor_and_inverse(sums, old, packed):
        count = old.shape[0]
        inverse = (message_rows(count, block), block) if packed else (count, block, block)
        return pl.pallas_call(
            functools.partial(factor_kernel, tokens, packed, count, block),
            out_shape=[shaped(old.shape, F32), shaped(inverse, BF16)],
            in_specs=[VMEM] * (len(sums) + 1),
            out_specs=[VMEM] * 2,
            compiler_params=params(24),
            cost_estimate=cost(2 * 45 * count * block ** 3 * 8, 4 * old.size),
            name="newton",
        )(*sums, old)

    count_in = old_in_factor.shape[1]
    count_out = old_out_factor.shape[1]
    in_sums = block_sums(acts, count_in)
    out_sums = block_sums(grads_out, count_out)
    in_factor, in_message = factor_and_inverse(in_sums, old_in_factor[0], True)
    messages = [in_message] + [lax.ppermute(in_message, "dp", ahead(k)) for k in range(1, chips)]
    messages = messages + [lax.ppermute(m, "dp", swap) for m in messages]
    out_factor, out_inverse = factor_and_inverse(out_sums, old_out_factor[0], False)

    wide = count_in * block
    fold = (message_rows(count_in, block), block)
    left, folds = pl.pallas_call(
        functools.partial(left_kernel, count_in, block),
        grid=(groups,),
        out_shape=[shaped((rows, width), BF16), shaped((groups,) + fold, F32)],
        in_specs=[
            pl.BlockSpec(out_inverse.shape, lambda i: (0, 0, 0)),
            pl.BlockSpec((rows, wide), lambda i: (0, i)),
        ],
        out_specs=[
            pl.BlockSpec((rows, wide), lambda i: (0, i)),
            pl.BlockSpec((1,) + fold, lambda i: (i, 0, 0)),
        ],
        compiler_params=params(24),
        cost_estimate=cost(4 * rows * width * block, 4 * rows * width),
        name="left",
    )(out_inverse, weight_grad[0])

    partial = pl.pallas_call(
        functools.partial(quad_kernel, chips),
        out_shape=shaped((8, block), F32),
        in_specs=[VMEM] * (groups + 1),
        out_specs=VMEM,
        compiler_params=params(24),
        cost_estimate=cost(folds.size, 4 * folds.size),
        name="quad",
    )(*messages, folds)
    for step in range(1, sections):
        ring = [(i, (i + step) % sections) for i in range(sections)]
        moved = lax.ppermute(partial, "section", ring)
        layer_sum = moved if step == 1 else layer_sum + moved
    partial = partial + layer_sum if sections > 1 else partial
    partials = [partial]
    for step in range(1, groups):
        ring = [(i, (i + step) % groups) for i in range(groups)]
        partials.append(lax.ppermute(partial, "dp", ring))

    natural = pl.pallas_call(
        functools.partial(natural_kernel, chips, count_in, block),
        out_shape=shaped((rows, width), F32),
        in_specs=[VMEM] * (groups + 1),
        out_specs=VMEM,
        compiler_params=params(24),
        cost_estimate=cost(2 * rows * width * block, 6 * rows * width),
        name="natural",
    )(*messages, left)

    tall = math.gcd(rows, 64)
    update = pl.pallas_call(
        functools.partial(scale_kernel, sections * rows * groups * width),
        grid=(rows // tall,),
        out_shape=shaped((rows, width), BF16),
        in_specs=[VMEM] * (groups + 1),
        out_specs=pl.BlockSpec((tall, width), lambda i: (i, 0)),
        compiler_params=params(24),
        cost_estimate=cost(rows * width, 6 * rows * width),
        name="scale",
    )(*partials, natural)
    return (update[None], in_factor[None], out_factor[None])


def solution(mesh):
    placed = (
        P("section", None, "dp", None),
        P("section", None, "dp", None),
        P("section", "dp", None),
        P("section", "dp", None, None),
        P("section", "dp", None, None),
    )
    return jax.shard_map(
        body,
        mesh=mesh,
        in_specs=placed,
        out_specs=(
            P("section", "dp", None),
            P("section", "dp", None, None),
            P("section", "dp", None, None),
        ),
        check_vma=False,
    )
```

```python
import functools
import math

import jax
import jax.numpy as jnp
from jax import lax
from jax.experimental import pallas as pl
from jax.experimental.pallas import tpu as pltpu
from jax.sharding import PartitionSpec as P

ITERS = 8
DECAY = 0.7
DAMPING = 0.1
CLIP = 0.04
F32 = jnp.float32
BF16 = jnp.bfloat16
VMEM = pl.BlockSpec(memory_space=pltpu.VMEM)


def pairs_of(count):
    pairs = [(b, b + 1) for b in range(0, count - 1, 2)]
    return pairs + ([(count - 1, None)] if count % 2 else [])


def message_rows(count, block):
    pairs = len(pairs_of(count))
    return pairs * block + -(-pairs // 16) * 16


def grid_of(block):
    rows = lax.broadcasted_iota(jnp.int32, (block, block), 0)
    cols = lax.broadcasted_iota(jnp.int32, (block, block), 1)
    return rows, cols


def contract_rows(a, b):
    return lax.dot_general(a, b, (((0,), (0,)), ((), ())), preferred_element_type=F32)


def dot(a, b):
    return jnp.dot(a, b, preferred_element_type=F32)


def pack(blocks, block):
    rows, cols = grid_of(block)
    pairs = pairs_of(len(blocks))
    extra = message_rows(len(blocks), block) - len(pairs) * block
    spot = lax.broadcasted_iota(jnp.int32, (extra, block), 0)
    tail = jnp.zeros((extra, block), F32)
    parts = []
    for at, (a, b) in enumerate(pairs):
        first = blocks[a]
        if b is None:
            parts.append(first)
            continue
        parts.append(jnp.where(rows < cols, first, blocks[b]))
        line = jnp.sum(jnp.where(rows == cols, first, 0.0), axis=0, keepdims=True)
        tail = jnp.where(spot == at, line, tail)
    return jnp.concatenate(parts + [tail], axis=0)


def unpacked(packed, count, block):
    rows, cols = grid_of(block)
    pairs = pairs_of(count)
    height = len(pairs) * block
    blocks = []
    for at, (a, b) in enumerate(pairs):
        joined = packed[at * block:(at + 1) * block]
        if b is None:
            blocks.append(joined)
            continue
        flipped = joined.T
        line = packed[height + at:height + at + 1]
        blocks.append(jnp.where(rows == cols, line, jnp.where(rows < cols, joined, flipped)))
        blocks.append(jnp.where(rows < cols, flipped, joined))
    return blocks


def gram_kernel(chips, counts, block, *refs):
    values, (out_ref,) = refs[:2], refs[-1:]
    base_ref = refs[2] if len(refs) == 4 else None
    core = lax.rem(lax.axis_index("dp"), 2)
    for step in range(chips):
        top = 0
        for ref, count in zip(values, counts):
            wide = count * block
            start = pl.multiple_of((step * 2 + core) * wide, wide)
            tokens = jnp.concatenate([ref[m, :, pl.ds(start, wide)] for m in range(ref.shape[0])], axis=0)
            grams = []
            for b in range(count):
                part = tokens[:, b * block:(b + 1) * block]
                grams.append(contract_rows(part, part))
            tall = message_rows(count, block)
            packed = pack(grams, block)
            if base_ref is not None:
                packed = packed + base_ref[step, top:top + tall]
            out_ref[step, top:top + tall] = packed.astype(out_ref.dtype)
            top += tall


def halves(x):
    high = x.astype(BF16)
    return high, (x - high.astype(F32)).astype(BF16)


def inverses(damped, block):
    rows, cols = grid_of(block)
    eye2 = jnp.where(rows == cols, 2.0, 0.0)
    norms = [jnp.sqrt(jnp.sum(m * m, axis=(0, 1), keepdims=True)) for m in damped]
    ys = [m / n for m, n in zip(damped, norms)]
    xs = [eye2 - y for y in ys]
    for stage in range(ITERS):
        parts = [halves(y) for y in ys]
        lefts = []
        for x, (high, low) in zip(xs, parts):
            if stage == 0:
                lefts.append((high, low))
                continue
            x_high, x_low = halves(x)
            if stage == ITERS - 1:
                lefts.append((x_high, x_low))
            else:
                lefts.append((jnp.concatenate([x_high, high], 0), jnp.concatenate([x_low, low], 0)))
        prods = []
        for (lhigh, llow), (high, low) in zip(lefts, parts):
            both = jnp.concatenate([lhigh, llow], 1)
            prods.append(dot(both, jnp.concatenate([high, high], 0)) + dot(lhigh, low))
        if stage == 0:
            ys = [2.0 * y - p for y, p in zip(ys, prods)]
        elif stage == ITERS - 1:
            xs = [2.0 * x - p for x, p in zip(xs, prods)]
        else:
            xs = [2.0 * x - p[:block] for x, p in zip(xs, prods)]
            ys = [2.0 * y - p[block:] for y, p in zip(ys, prods)]
    return [x / n for x, n in zip(xs, norms)]


def factor_kernel(tokens, block, sums_ref, old_in_ref, old_out_ref, in_ref, out_ref, message_ref, inverse_ref):
    total = sums_ref[0]
    for step in range(1, sums_ref.shape[0]):
        total = total + sums_ref[step]
    rows, cols = grid_of(block)
    damped, top = [], 0
    for old_ref, factor_ref in ((old_in_ref, in_ref), (old_out_ref, out_ref)):
        count = old_ref.shape[0]
        tall = message_rows(count, block)
        for b, gram in enumerate(unpacked(total[top:top + tall], count, block)):
            factor = DECAY * old_ref[b] + ((1.0 - DECAY) / tokens) * gram
            factor_ref[b] = factor
            damped.append(factor + jnp.where(rows == cols, DAMPING, 0.0))
        top += tall
    results = inverses(damped, block)
    count = old_in_ref.shape[0]
    message = pack(results[:count], block).astype(BF16)
    for step in range(message_ref.shape[0]):
        message_ref[step] = message
    for b, inverse in enumerate(results[count:]):
        inverse_ref[b] = inverse.astype(BF16)


def left_kernel(count, block, inverse_ref, grad_ref, left_ref, fold_ref):
    outs = inverse_ref.shape[0]
    rows, cols = grid_of(block)
    grad = grad_ref[...]
    left = jnp.concatenate([
        dot(inverse_ref[b], grad[b * block:(b + 1) * block]).astype(BF16) for b in range(outs)
    ], axis=0)
    left_ref[...] = left
    sums = []
    for c in range(count):
        span = slice(c * block, (c + 1) * block)
        sums.append(contract_rows(left[:, span], grad[:, span]))
    pairs = pairs_of(count)
    height = len(pairs) * block
    extra = fold_ref.shape[1] - height
    tail = jnp.zeros((extra, block), F32)
    spot = lax.broadcasted_iota(jnp.int32, (extra, block), 0)
    for at, (a, b) in enumerate(pairs):
        first = sums[a]
        if b is None:
            fold_ref[0, at * block:(at + 1) * block, :] = first
            continue
        second = sums[b]
        fold_ref[0, at * block:(at + 1) * block, :] = jnp.where(
            rows < cols, first + first.T, second + jnp.where(rows > cols, second.T, 0.0)
        )
        line = jnp.sum(jnp.where(rows == cols, first, 0.0), axis=0, keepdims=True)
        tail = jnp.where(spot == at, line, tail)
    fold_ref[0, height:, :] = tail


def owner_of(side, chip):
    return chip * 2 + lax.rem(lax.axis_index("dp") + side, 2)


def quad_kernel(chips, *refs):
    messages, (fold_ref, out_ref) = refs[:-2], refs[-2:]
    total = None
    for side, ref in enumerate(messages):
        for chip in range(chips):
            term = ref[chip].astype(F32) * fold_ref[owner_of(side, chip)]
            total = term if total is None else total + term
    out_ref[...] = jnp.broadcast_to(jnp.sum(total, axis=(0, 1), keepdims=True)[None], out_ref.shape)


def natural_kernel(chips, count, block, *refs):
    messages, (left_ref, out_ref) = refs[:-2], refs[-2:]
    for side, chip in ((side, chip) for side in range(2) for chip in range(chips)):
        start = owner_of(side, chip) * (count * block)
        for b, inverse in enumerate(unpacked(messages[side][chip].astype(F32), count, block)):
            cols = pl.ds(pl.multiple_of(start + b * block, block), block)
            out_ref[:, cols] = dot(left_ref[:, cols], inverse.astype(BF16))


def scale_kernel(numel, *refs):
    sums_ref, natural_ref, out_ref = refs
    quad = sums_ref[0]
    for step in range(1, sums_ref.shape[0]):
        quad = quad + sums_ref[step]
    scale = jnp.minimum(1.0, jnp.sqrt(CLIP * numel / quad))[0:1, 0:1]
    tall = out_ref.shape[0]
    rows = pl.ds(pl.multiple_of(pl.program_id(0) * tall, tall), tall)
    out_ref[...] = (scale * natural_ref[rows, :]).astype(BF16)


def cost(flops, size):
    return pl.CostEstimate(flops=int(flops), bytes_accessed=int(size), transcendentals=0)


def params(mib):
    return pltpu.CompilerParams(vmem_limit_bytes=mib << 20)


def shaped(shape, dtype):
    return jax.ShapeDtypeStruct(shape, dtype)


def body(acts, grads_out, weight_grad, old_in_factor, old_out_factor):
    groups = lax.axis_size("dp")
    sections = lax.axis_size("section")
    chips = groups // 2
    block = old_in_factor.shape[-1]
    rows, width = weight_grad.shape[1:]
    tokens = acts.shape[1] * acts.shape[2] * groups

    swap = [(i, i ^ 1) for i in range(groups)]

    along_chips = [[c * 2 + core for c in range(chips)] for core in range(2)]

    counts = (old_in_factor.shape[1], old_out_factor.shape[1])
    talls = [message_rows(count, block) for count in counts]
    others = [lax.ppermute(values, "dp", swap)[0] for values in (acts, grads_out)]

    def gram(*values):
        return pl.pallas_call(
            functools.partial(gram_kernel, chips, counts, block),
            out_shape=shaped((chips, sum(talls), block), F32),
            in_specs=[VMEM] * len(values),
            out_specs=VMEM,
            compiler_params=params(24),
            cost_estimate=cost(2 * tokens // groups * block * width, 4 * acts.size),
            name="gram",
        )(*values)

    sums = gram(*others, gram(acts[0], grads_out[0]))
    sums = lax.all_to_all(sums.astype(jnp.float16), "dp", 0, 0, axis_index_groups=along_chips, tiled=True)
    in_factor, out_factor, in_message, out_inverse = pl.pallas_call(
        functools.partial(factor_kernel, tokens, block),
        out_shape=[
            shaped(old_in_factor.shape[1:], F32),
            shaped(old_out_factor.shape[1:], F32),
            shaped((chips, talls[0], block), BF16),
            shaped(old_out_factor.shape[1:], BF16),
        ],
        in_specs=[VMEM] * 3,
        out_specs=[VMEM] * 4,
        compiler_params=params(24),
        cost_estimate=cost(90 * sum(counts) * block ** 3, 12 * old_in_factor.size),
        name="newton",
    )(sums.astype(F32), old_in_factor[0], old_out_factor[0])
    count_in = counts[0]
    near = lax.all_to_all(in_message, "dp", 0, 0, axis_index_groups=along_chips, tiled=True)
    messages = [near, lax.ppermute(near, "dp", swap)]

    wide = count_in * block
    fold = (message_rows(count_in, block), block)
    left, folds = pl.pallas_call(
        functools.partial(left_kernel, count_in, block),
        grid=(groups,),
        out_shape=[shaped((rows, width), BF16), shaped((groups,) + fold, F32)],
        in_specs=[
            pl.BlockSpec(out_inverse.shape, lambda i: (0, 0, 0)),
            pl.BlockSpec((rows, wide), lambda i: (0, i)),
        ],
        out_specs=[
            pl.BlockSpec((rows, wide), lambda i: (0, i)),
            pl.BlockSpec((1,) + fold, lambda i: (i, 0, 0)),
        ],
        compiler_params=params(24),
        cost_estimate=cost(4 * rows * width * block, 4 * rows * width),
        name="left",
    )(out_inverse, weight_grad[0])

    partial = pl.pallas_call(
        functools.partial(quad_kernel, chips),
        out_shape=shaped((sections * groups, 8, block), F32),
        in_specs=[VMEM] * 3,
        out_specs=VMEM,
        compiler_params=params(24),
        cost_estimate=cost(folds.size, 4 * folds.size),
        name="quad",
    )(*messages, folds)
    partials = lax.all_to_all(partial, ("section", "dp"), 0, 0, tiled=True)

    natural = pl.pallas_call(
        functools.partial(natural_kernel, chips, count_in, block),
        out_shape=shaped((rows, width), F32),
        in_specs=[VMEM] * 3,
        out_specs=VMEM,
        compiler_params=params(24),
        cost_estimate=cost(2 * rows * width * block, 6 * rows * width),
        name="natural",
    )(*messages, left)

    tall = math.gcd(rows, 64)
    update = pl.pallas_call(
        functools.partial(scale_kernel, sections * rows * groups * width),
        grid=(rows // tall,),
        out_shape=shaped((rows, width), BF16),
        in_specs=[VMEM] * 2,
        out_specs=pl.BlockSpec((tall, width), lambda i: (i, 0)),
        compiler_params=params(24),
        cost_estimate=cost(rows * width, 6 * rows * width),
        name="scale",
    )(partials, natural)
    return (update[None], in_factor[None], out_factor[None])


def solution(mesh):
    placed = (
        P("section", None, "dp", None),
        P("section", None, "dp", None),
        P("section", "dp", None),
        P("section", "dp", None, None),
        P("section", "dp", None, None),
    )
    return jax.shard_map(
        body,
        mesh=mesh,
        in_specs=placed,
        out_specs=(
            P("section", "dp", None),
            P("section", "dp", None, None),
            P("section", "dp", None, None),
        ),
        check_vma=False,
    )
```

```python
import functools
import math

import jax
import jax.numpy as jnp
from jax import lax
from jax.experimental import pallas as pl
from jax.experimental.pallas import tpu as pltpu
from jax.sharding import PartitionSpec as P

ITERS = 8
DECAY = 0.7
DAMPING = 0.1
CLIP = 0.04
F32 = jnp.float32
BF16 = jnp.bfloat16
F16 = jnp.float16
VMEM = pl.BlockSpec(memory_space=pltpu.VMEM)


def pairs_of(count):
    pairs = [(b, b + 1) for b in range(0, count - 1, 2)]
    return pairs + ([(count - 1, None)] if count % 2 else [])


def message_rows(count, block):
    pairs = len(pairs_of(count))
    return pairs * block + -(-pairs // 16) * 16


def grid_of(block):
    rows = lax.broadcasted_iota(jnp.int32, (block, block), 0)
    cols = lax.broadcasted_iota(jnp.int32, (block, block), 1)
    return rows, cols


def contract_rows(a, b):
    return lax.dot_general(a, b, (((0,), (0,)), ((), ())), preferred_element_type=F32)


def dot(a, b):
    return jnp.dot(a, b, preferred_element_type=F32)


def pack(blocks, block):
    rows, cols = grid_of(block)
    pairs = pairs_of(len(blocks))
    extra = message_rows(len(blocks), block) - len(pairs) * block
    spot = lax.broadcasted_iota(jnp.int32, (extra, block), 0)
    tail = jnp.zeros((extra, block), F32)
    parts = []
    for at, (a, b) in enumerate(pairs):
        first = blocks[a]
        if b is None:
            parts.append(first)
            continue
        parts.append(jnp.where(rows < cols, first, blocks[b]))
        line = jnp.sum(jnp.where(rows == cols, first, 0.0), axis=0, keepdims=True)
        tail = jnp.where(spot == at, line, tail)
    return jnp.concatenate(parts + [tail], axis=0)


def unpacked(packed, count, block):
    rows, cols = grid_of(block)
    pairs = pairs_of(count)
    height = len(pairs) * block
    blocks = []
    for at, (a, b) in enumerate(pairs):
        joined = packed[at * block:(at + 1) * block]
        if b is None:
            blocks.append(joined)
            continue
        flipped = joined.T
        line = packed[height + at:height + at + 1]
        blocks.append(jnp.where(rows == cols, line, jnp.where(rows < cols, joined, flipped)))
        blocks.append(jnp.where(rows < cols, flipped, joined))
    return blocks


def partner(step, size):
    if size & (size - 1) == 0:
        return lambda place: place ^ step
    return lambda place: (place + step) % size


def gram_kernel(chips, count, block, values_ref, *refs):
    bases, outs = refs[:-chips], refs[-chips:]
    place = lax.axis_index("dp")
    chip, core = place // 2, lax.rem(place, 2)
    wide = count * block
    for step in range(chips):
        met = chip ^ step if chips & (chips - 1) == 0 else lax.rem(chip + step, chips)
        start = pl.multiple_of((met * 2 + core) * wide, wide)
        tokens = jnp.concatenate([values_ref[m, :, pl.ds(start, wide)] for m in range(values_ref.shape[0])], axis=0)
        grams = []
        for b in range(count):
            part = tokens[:, b * block:(b + 1) * block]
            grams.append(contract_rows(part, part))
        packed = pack(grams, block)
        outs[step][...] = packed + bases[step][...] if bases else packed


def halves(x):
    high = x.astype(BF16)
    return high, (x - high.astype(F32)).astype(BF16)


def inverses(damped, block):
    rows, cols = grid_of(block)
    eye2 = jnp.where(rows == cols, 2.0, 0.0)
    norms = [jnp.sqrt(jnp.sum(m * m, axis=(0, 1), keepdims=True)) for m in damped]
    ys = [m / n for m, n in zip(damped, norms)]
    xs = [eye2 - y for y in ys]
    for stage in range(ITERS):
        parts = [halves(y) for y in ys]
        lefts = []
        for x, (high, low) in zip(xs, parts):
            if stage == 0:
                lefts.append((high, low))
                continue
            x_high, x_low = halves(x)
            if stage == ITERS - 1:
                lefts.append((x_high, x_low))
            else:
                lefts.append((jnp.concatenate([x_high, high], 0), jnp.concatenate([x_low, low], 0)))
        prods = []
        for (lhigh, llow), (high, low) in zip(lefts, parts):
            both = jnp.concatenate([lhigh, llow], 1)
            prods.append(dot(both, jnp.concatenate([high, high], 0)) + dot(lhigh, low))
        if stage == 0:
            ys = [2.0 * y - p for y, p in zip(ys, prods)]
        elif stage == ITERS - 1:
            xs = [2.0 * x - p for x, p in zip(xs, prods)]
        else:
            xs = [2.0 * x - p[:block] for x, p in zip(xs, prods)]
            ys = [2.0 * y - p[block:] for y, p in zip(ys, prods)]
    return [x / n for x, n in zip(xs, norms)]


def factor_kernel(tokens, packed, block, sum_ref, old_ref, factor_ref, inverse_ref):
    count = old_ref.shape[0]
    rows, cols = grid_of(block)
    damped = []
    for b, gram in enumerate(unpacked(sum_ref[...], count, block)):
        factor = DECAY * old_ref[b] + ((1.0 - DECAY) / tokens) * gram
        factor_ref[b] = factor
        damped.append(factor + jnp.where(rows == cols, DAMPING, 0.0))
    results = inverses(damped, block)
    if packed:
        inverse_ref[...] = pack(results, block).astype(BF16)
    else:
        for b, inverse in enumerate(results):
            inverse_ref[b] = inverse.astype(BF16)


def left_kernel(count, block, inverse_ref, grad_ref, left_ref, fold_ref):
    outs = inverse_ref.shape[0]
    rows, cols = grid_of(block)
    wide = count * block
    pairs = pairs_of(count)
    height = len(pairs) * block
    extra = fold_ref.shape[1] - height
    spot = lax.broadcasted_iota(jnp.int32, (extra, block), 0)

    def owner(at, carry):
        span = pl.ds(pl.multiple_of(at * wide, wide), wide)
        grad = grad_ref[:, span]
        left = jnp.concatenate([
            dot(inverse_ref[b], grad[b * block:(b + 1) * block]).astype(BF16) for b in range(outs)
        ], axis=0)
        left_ref[:, span] = left
        sums = []
        for c in range(count):
            part = slice(c * block, (c + 1) * block)
            sums.append(contract_rows(left[:, part], grad[:, part]))
        tail = jnp.zeros((extra, block), F32)
        for index, (a, b) in enumerate(pairs):
            first = sums[a]
            here = slice(index * block, (index + 1) * block)
            if b is None:
                fold_ref[at, here, :] = first
                continue
            second = sums[b]
            fold_ref[at, here, :] = jnp.where(
                rows < cols, first + first.T, second + jnp.where(rows > cols, second.T, 0.0)
            )
            line = jnp.sum(jnp.where(rows == cols, first, 0.0), axis=0, keepdims=True)
            tail = jnp.where(spot == index, line, tail)
        fold_ref[at, height:, :] = tail
        return carry

    lax.fori_loop(0, fold_ref.shape[0], owner, 0)


def owner_of(index, chips):
    place = lax.axis_index("dp")
    chip, core = place // 2, lax.rem(place, 2)
    side, step = index // chips, index % chips
    met = chip ^ step if chips & (chips - 1) == 0 else lax.rem(chip + chips - step, chips)
    return met * 2 + (core if side == 0 else 1 - core)


def quad_kernel(chips, *refs):
    messages, (fold_ref, out_ref) = refs[:-2], refs[-2:]
    total = None
    for index, ref in enumerate(messages):
        term = ref[...].astype(F32) * fold_ref[owner_of(index, chips)]
        total = term if total is None else total + term
    out_ref[...] = jnp.broadcast_to(jnp.sum(total, axis=(0, 1), keepdims=True), out_ref.shape)


def natural_kernel(chips, count, block, *refs):
    messages, (left_ref, out_ref) = refs[:-2], refs[-2:]
    for index, ref in enumerate(messages):
        start = owner_of(index, chips) * (count * block)
        for b, inverse in enumerate(unpacked(ref[...].astype(F32), count, block)):
            cols = pl.ds(pl.multiple_of(start + b * block, block), block)
            out_ref[:, cols] = dot(left_ref[:, cols], inverse.astype(BF16))


def scale_kernel(numel, quad_ref, natural_ref, out_ref, held_ref, sems):
    scale = jnp.minimum(1.0, jnp.sqrt(CLIP * numel / quad_ref[...]))[0:1, 0:1]
    parts = sems.shape[0]
    tall = out_ref.shape[0] // parts
    copies = []
    for at in range(parts):
        rows = pl.ds(at * tall, tall)
        held_ref[rows, :] = (scale * natural_ref[rows, :]).astype(BF16)
        copies.append(pltpu.make_async_copy(held_ref.at[rows, :], out_ref.at[rows, :], sems.at[at]))
        copies[-1].start()
    for copy in copies:
        copy.wait()


def cost(flops, size):
    return pl.CostEstimate(flops=int(flops), bytes_accessed=int(size), transcendentals=0)


def params(mib):
    return pltpu.CompilerParams(vmem_limit_bytes=mib << 20)


def shaped(shape, dtype):
    return jax.ShapeDtypeStruct(shape, dtype)


def body(acts, grads_out, weight_grad, old_in_factor, old_out_factor):
    groups = lax.axis_size("dp")
    sections = lax.axis_size("section")
    chips = groups // 2
    block = old_in_factor.shape[-1]
    rows, width = weight_grad.shape[1:]
    tokens = acts.shape[1] * acts.shape[2] * groups

    swap = [(i, i ^ 1) for i in range(groups)]

    meets = [partner(step, chips) for step in range(chips)]

    def met(step):
        return [(c * 2 + core, meets[step](c) * 2 + core) for c in range(chips) for core in range(2)]

    def block_sums(values, count):
        other = lax.ppermute(values, "dp", swap)
        shape = (message_rows(count, block), block)

        def gram(part, bases):
            return pl.pallas_call(
                functools.partial(gram_kernel, chips, count, block),
                out_shape=[shaped(shape, F32)] * chips,
                in_specs=[VMEM] * (1 + len(bases)),
                out_specs=[VMEM] * chips,
                compiler_params=params(16),
                cost_estimate=cost(tokens // groups * block * width, 2 * values.size),
                name="gram",
            )(part, *bases)

        sums = gram(other[0], gram(values[0], ()))
        total = sums[0]
        moved = [lax.ppermute(sums[k].astype(F16), "dp", met(k)) for k in range(1, chips)]
        for part in moved:
            total = total + part.astype(F32)
        return total

    def factor_and_inverse(total, old, packed):
        count = old.shape[0]
        inverse = (message_rows(count, block), block) if packed else (count, block, block)
        return pl.pallas_call(
            functools.partial(factor_kernel, tokens, packed, block),
            out_shape=[shaped(old.shape, F32), shaped(inverse, BF16)],
            in_specs=[VMEM] * 2,
            out_specs=[VMEM] * 2,
            compiler_params=params(16),
            cost_estimate=cost(90 * count * block ** 3, 12 * old.size),
            name="newton",
        )(total, old)

    def sum_over(value, axis, size):
        if size & (size - 1) == 0:
            bit = 1
            while bit < size:
                value = value + lax.ppermute(value, axis, [(i, i ^ bit) for i in range(size)])
                bit *= 2
            return value
        parts = [lax.ppermute(value, axis, [(i, (i + k) % size) for i in range(size)]) for k in range(1, size)]
        return functools.reduce(jnp.add, parts, value)

    count_in = old_in_factor.shape[1]
    count_out = old_out_factor.shape[1]
    in_sum = block_sums(acts, count_in)
    out_sum = block_sums(grads_out, count_out)
    in_factor, in_message = factor_and_inverse(in_sum, old_in_factor[0], True)
    messages = [in_message] + [lax.ppermute(in_message, "dp", met(k)) for k in range(1, chips)]
    messages = messages + [lax.ppermute(m, "dp", swap) for m in messages]
    out_factor, out_inverse = factor_and_inverse(out_sum, old_out_factor[0], False)

    fold = (groups, message_rows(count_in, block), block)
    left, folds = pl.pallas_call(
        functools.partial(left_kernel, count_in, block),
        out_shape=[shaped((rows, width), BF16), shaped(fold, F32)],
        in_specs=[VMEM] * 2,
        out_specs=[VMEM] * 2,
        compiler_params=params(16),
        cost_estimate=cost(4 * rows * width * block, 4 * rows * width),
        name="left",
    )(out_inverse, weight_grad[0])

    quad = pl.pallas_call(
        functools.partial(quad_kernel, chips),
        out_shape=shaped((8, block), F32),
        in_specs=[VMEM] * (groups + 1),
        out_specs=VMEM,
        compiler_params=params(16),
        cost_estimate=cost(folds.size, 4 * folds.size),
        name="quad",
    )(*messages, folds)
    quad = sum_over(sum_over(quad, "section", sections), "dp", groups)

    natural = pl.pallas_call(
        functools.partial(natural_kernel, chips, count_in, block),
        out_shape=shaped((rows, width), F32),
        in_specs=[VMEM] * (groups + 1),
        out_specs=VMEM,
        compiler_params=params(16),
        cost_estimate=cost(2 * rows * width * block, 6 * rows * width),
        name="natural",
    )(*messages, left)

    parts = rows // math.gcd(rows, 32)
    update = pl.pallas_call(
        functools.partial(scale_kernel, sections * rows * groups * width),
        out_shape=shaped((rows, width), BF16),
        in_specs=[VMEM] * 2,
        out_specs=pl.BlockSpec(memory_space=pl.ANY),
        scratch_shapes=[pltpu.VMEM((rows, width), BF16), pltpu.SemaphoreType.DMA((parts,))],
        compiler_params=params(16),
        cost_estimate=cost(rows * width, 6 * rows * width),
        name="scale",
    )(quad, natural)
    return (update[None], in_factor[None], out_factor[None])


def solution(mesh):
    placed = (
        P("section", None, "dp", None),
        P("section", None, "dp", None),
        P("section", "dp", None),
        P("section", "dp", None, None),
        P("section", "dp", None, None),
    )
    return jax.shard_map(
        body,
        mesh=mesh,
        in_specs=placed,
        out_specs=(
            P("section", "dp", None),
            P("section", "dp", None, None),
            P("section", "dp", None, None),
        ),
        check_vma=False,
    )
```
